32 devices in a mesh: grp: 2 (over x), ex: 16 (over z, y, core).
Axes of the slice: x: 2, y: 2, z: 4, core: 2. Of those that a mesh axis runs over, the one named last changes fastest.
Arguments:
- queries: bfloat16 [2, 32, 4, 1536], P(None, ('grp', 'ex')), parts along dimension 1, may hold values from -8 to 8
- keys: bfloat16 [2, 32, 4, 2, 256, 128], P(None, ('grp', 'ex')), parts along dimension 1, may hold values from -8 to 8
- values: bfloat16 [2, 32, 4, 2, 256, 128], P(None, ('grp', 'ex')), parts along dimension 1, may hold values from -6 to 6
- lengths: int32 [2, 32], P(None, ('grp', 'ex')), parts along dimension 1, may hold values from 1 to 256, 2048 in all within a row
- routes: int32 [2, 32, 4], P(None, ('grp', 'ex')), parts along dimension 1, may hold values from 0 to 7, all different within a row
- residual: bfloat16 [2, 32, 6144], P(None, ('grp', 'ex')), parts along dimension 1, may hold values from -6 to 6
- gain: bfloat16 [6144], replicated, may hold values from 0.099609375 to 1.8984375
- w_router: bfloat16 [6144, 8], replicated, may hold values from -0.3125 to 0.3125
- w_in: bfloat16 [16, 6144, 2688], P('ex'), may hold values from -0.078125 to 0.078125
- w_out: bfloat16 [16, 2688, 6144], P('ex'), may hold values from -0.078125 to 0.078125
Outputs:
- layer_out: bfloat16 [2, 32, 6144], P(None, ('grp', 'ex')), parts along dimension 1
The draws below stay inside these ranges and needn't reach their ends.
There are 2 independent parts, one for each index of `grp`. The reference program is written for one: setup_inputs(seed, part) draws one part's arguments, and reference() takes and returns one part's arrays. A program takes and returns all parts, laid end to end along the dimension named above; an argument that names none is the same for every part. Nothing has to cross between parts.
Inputs may be any that keep to these rules, and one draw needn't show every extreme that they name: `routes`: each row names 4 different experts. The lengths of the rows of each micro-batch sum to 2048, and in each micro-batch some row uses all 256 positions.
All inputs are finite; a program needn't handle non-finite values. No bound on the sum of `lengths` on one device may be relied on, other than what follows from the above.
Results may differ from the reference program's by a relative error of at most 0.0045.
Values may be sent and summed in bfloat16 or wider, within the bound.
A program may use at most 192 MiB of HBM per device.

```python
import math
import jax
import jax.numpy as jnp
import numpy as np
from jax import lax

HD = 128
D = 6144
HQ_DEV = 12
KV_DEV = 2
FF = 5376
EXPERTS = 8
TOP = 4
ESPLIT = 2
FF_DEV = 2688
L = 256
MB = 2
GROUP_ROWS = 4
SHARDS = 16
ROWS_MB = 16


def draw_queries(key, part):
    key = jax.random.fold_in(key, 11)
    return jnp.clip(jax.random.normal(key, (MB, SHARDS, GROUP_ROWS, HQ_DEV * HD), jnp.float32), -4.0, 4.0).astype(jnp.bfloat16)


def draw_keys(key, part):
    key = jax.random.fold_in(key, 12)
    shape = (MB, SHARDS, GROUP_ROWS, KV_DEV, L, HD)
    return jnp.clip(jax.random.normal(key, shape, jnp.float32), -4.0, 4.0).astype(jnp.bfloat16)


def block_scale(own_key, dims, cuts, least, largest):
    loudness, own = 1.0, jax.random.fold_in(own_key, 6)
    for dim, blocks in cuts:
        heights = jnp.exp(jax.random.uniform(jax.random.fold_in(own, dim), (blocks,), jnp.float32, least / len(cuts), largest / len(cuts)))
        loudness = loudness * jnp.repeat(heights, dims[dim] // blocks).reshape([-1 if axis == dim else 1 for axis in range(len(dims))])
    return loudness


def distinct(own_key, rows, count, top, lift):
    ranking = jax.random.permutation(jax.random.fold_in(own_key, 1), count)
    favour = ranking
    for power in range(3):
        favour = favour * favour // count
    favour = favour * lift // count
    lots = jax.random.randint(jax.random.fold_in(own_key, 2), (rows, count), 0, 4096) + favour
    sure = jax.random.permutation(jax.random.fold_in(own_key, 3), rows)[jnp.arange(count) % rows]
    lots = jnp.where(jnp.arange(rows)[:, None] == sure[None, :], 1 << 14, lots)
    score = lots * count + jnp.arange(count)
    return lax.top_k(score.astype(jnp.int32), top)[1].astype(jnp.int32)


def length_profile(number_of, total, reach, lean):
    loads = [(1 << 20) // math.isqrt(grade ** lean) + 1 for grade in range(2, number_of + 1)]
    surplus, holding = total - reach - (number_of - 1), [1] * (number_of - 1)
    while surplus > 0:
        free = [i for i in range(number_of - 1) if holding[i] < reach]
        whole, left = sum([loads[i] for i in free]), surplus
        for i in free:
            more = min(reach - holding[i], max(1, left * loads[i] // whole), surplus)
            holding[i] = holding[i] + more
            surplus = surplus - more
    return np.array([reach] + holding)


def uneven_parts(own_key, number_of, total, limit, lean):
    if number_of == 2:
        one = jax.random.randint(own_key, (), max(1, total - limit), min(limit, total - 1) + 1)
        return jnp.stack([one, total - one])
    sizes = jnp.asarray(length_profile(number_of, total, limit, lean), jnp.int32)
    twos = (number_of - 1) // 2
    donor, receiver = sizes[1:1 + 2 * twos:2], sizes[2:2 + 2 * twos:2]
    room = jnp.minimum(donor - 1, limit - receiver)
    moved = jax.random.randint(jax.random.fold_in(own_key, 1), (twos,), 0, 1 << 20) % (room + 1)
    sizes = sizes.at[1:1 + 2 * twos:2].set(donor - moved).at[2:2 + 2 * twos:2].set(receiver + moved)
    return sizes[jax.random.permutation(jax.random.fold_in(own_key, 2), number_of)]


def normal_values(key, extent, spread, reach, cuts=(), kind=jnp.bfloat16):
    loudness = block_scale(key, extent, cuts, -0.22, 0.18) if cuts else 1.0
    drawn = jax.random.normal(key, extent, jnp.float32) * spread * loudness
    return jnp.minimum(jnp.maximum(drawn, -reach), reach).astype(kind)


def setup_inputs(seed: int = 0, part: int = 0) -> dict:
    key_list = jax.random.split(jax.random.key(seed), 11)
    part_splits = jax.random.split(jax.random.fold_in(key_list[10], part), 11)
    queries = draw_queries(jax.random.fold_in(jax.random.fold_in(key_list[10], part), 71), part)
    keys = draw_keys(jax.random.fold_in(jax.random.fold_in(key_list[10], part), 71), part)
    values = normal_values(part_splits[2], (MB, SHARDS, GROUP_ROWS, KV_DEV, L, HD), 1.0, 6.0, ((1, 16),))
    lengths = jax.vmap(lambda own: uneven_parts(own, ROWS_MB, ROWS_MB * (L // 2), L, 2))(jax.random.split(part_splits[3], MB)).reshape((MB, ROWS_MB)).astype(jnp.int32)
    routes = distinct(part_splits[4], MB * ROWS_MB, EXPERTS, TOP, 8192).reshape((MB, ROWS_MB, TOP))
    residual = normal_values(part_splits[5], (MB, ROWS_MB, D), 1.0, 6.0, ((1, 16),))
    gain = jnp.clip(1.0 + 0.18 * jax.random.normal(key_list[6], (D,), jnp.float32), 0.099609375, 1.8984375).astype(jnp.bfloat16)
    w_router = normal_values(key_list[7], (D, EXPERTS), (D // 16) ** -0.5, 0.3125)
    w_in = normal_values(key_list[8], (SHARDS, D, FF_DEV), D ** -0.5, 0.078125, ((0, 16),))
    w_out = normal_values(key_list[9], (SHARDS, FF_DEV, D), FF ** -0.5, 0.078125, ((0, 16),))
    return {"queries": queries, "keys": keys, "values": values, "lengths": lengths, "routes": routes, "residual": residual, "gain": gain, "w_router": w_router, "w_in": w_in, "w_out": w_out}


def reference(queries, keys, values, lengths, routes, residual, gain, w_router, w_in, w_out):
    groups_all = SHARDS // 4
    per_kv = HQ_DEV // KV_DEV
    full_in = w_in.reshape(EXPERTS, ESPLIT, D, FF_DEV).transpose(0, 2, 1, 3).reshape(EXPERTS, D, FF)
    full_out = w_out.reshape(EXPERTS, FF, D)
    results = []
    for micro in range(MB):
        query_heads = queries[micro].astype(jnp.float32).reshape(SHARDS, GROUP_ROWS, KV_DEV, per_kv, HD)
        scores = jnp.einsum('sgkqd,sgkld->sgkql', query_heads, keys[micro].astype(jnp.float32), precision=lax.Precision.HIGHEST) / math.sqrt(HD)
        span_len = jnp.repeat(lengths[micro].reshape(groups_all, GROUP_ROWS), 4, axis=0)
        position = jnp.arange(L, dtype=jnp.int32)
        valid = position[None, None, None, None, :] < span_len[:, :, None, None, None]
        masked = jnp.where(valid, scores, -1e+30)
        top = lax.optimization_barrier(jnp.max(masked, axis=-1, keepdims=True))
        expo = jnp.where(valid, jnp.exp(masked - top), 0.0)
        probs = (expo / lax.optimization_barrier(jnp.sum(expo, axis=-1, keepdims=True))).astype(jnp.bfloat16)
        context = jnp.einsum('sgkql,sgkld->sgkqd', probs.astype(jnp.float32), values[micro].astype(jnp.float32), precision=lax.Precision.HIGHEST)
        context = context.astype(jnp.bfloat16).reshape(groups_all, 4, GROUP_ROWS, HQ_DEV * HD)
        context = context.transpose(0, 2, 1, 3).reshape(ROWS_MB, D)
        state = residual[micro].astype(jnp.float32) + context.astype(jnp.float32)
        scale = lax.rsqrt(lax.optimization_barrier(jnp.mean(state * state, axis=-1, keepdims=True)) + 1e-05)
        normed = (state * scale * gain.astype(jnp.float32)).astype(jnp.bfloat16)
        logits = jnp.dot(normed, w_router, preferred_element_type=jnp.float32)
        chosen = routes[micro][:, :, None] == jnp.arange(EXPERTS, dtype=jnp.int32)[None, None, :]
        picked = lax.optimization_barrier(jnp.sum(jnp.where(chosen, logits[:, None, :], 0.0), axis=-1))
        gates = jax.nn.sigmoid(picked)
        shares = gates / lax.optimization_barrier(jnp.sum(gates, axis=-1, keepdims=True))
        mix = lax.optimization_barrier(jnp.sum(jnp.where(chosen, shares[:, :, None], 0.0), axis=1))

        def one_expert(pair):
            weight_in, weight_out = pair
            hidden = jax.nn.silu(jnp.dot(normed, weight_in, preferred_element_type=jnp.float32)).astype(jnp.bfloat16)
            return jnp.dot(hidden, weight_out, preferred_element_type=jnp.float32)
        expert_out = lax.map(one_expert, (full_in, full_out))
        mixed = state + lax.optimization_barrier(jnp.sum(mix.T[:, :, None] * expert_out, axis=0))
        results.append(mixed.astype(jnp.bfloat16))
    return jnp.stack(results, axis=0)
```

```python
import functools
import math

import jax
import jax.numpy as jnp
from jax import lax
from jax.experimental import pallas as pl
from jax.experimental.pallas import tpu as pltpu
from jax.sharding import PartitionSpec as P

HD = 128
EXPERTS = 8
BLOCKS = 8
OUT_SLOTS = 5
F32 = jnp.float32
BF16 = jnp.bfloat16


def layer_kernel(
    width,
    q_ref,
    len_ref,
    routes_ref,
    res_ref,
    gain_ref,
    k_hbm,
    v_hbm,
    wr_hbm,
    win_hbm,
    wout_hbm,
    out_ref,
    kbuf,
    vbuf,
    wrbuf,
    winbuf,
    woutbuf,
    lenbuf,
    ctx_out,
    ctx_in,
    gath,
    xbuf,
    hacc,
    hid,
    ykeep,
    pout,
    pin,
    rbuf,
    rin,
    kv_sem,
    win_sem,
    wout_sem,
    len_send,
    len_recv,
    ctx_send,
    ctx_recv,
    ag_send,
    ag_recv,
    fw_send,
    fw_recv,
    pair_send,
    pair_recv,
    ret_send,
    ret_recv,
):
    me = lax.axis_index("ex")
    chips = width // 2
    chip = me // 2
    core = me % 2
    quarter = me % 4
    base = me - quarter
    sibling = me + 1 - 2 * core
    blk = gain_ref.shape[1]
    half = width
    slots = woutbuf.shape[0]

    def same_core(offset):
        return lax.rem(chip + offset, chips) * 2 + core

    def remote(src, dst, send, recv, target):
        return pltpu.make_async_remote_copy(
            src_ref=src,
            dst_ref=dst,
            send_sem=send,
            recv_sem=recv,
            device_id={"ex": target},
            device_id_type=pl.DeviceIdType.MESH,
        )

    barrier = pltpu.get_barrier_semaphore()
    diagonal = base + 3 - quarter

    def greet(device):
        pl.semaphore_signal(
            barrier, inc=1, device_id={"ex": device}, device_id_type=pl.DeviceIdType.MESH
        )

    @pl.loop(1, chips)
    def _(offset):
        greet(same_core(offset))

    greet(sibling)
    greet(diagonal)

    kcopy = pltpu.make_async_copy(k_hbm, kbuf, kv_sem.at[0])
    vcopy = pltpu.make_async_copy(v_hbm, vbuf, kv_sem.at[1])
    wrcopy = pltpu.make_async_copy(wr_hbm, wrbuf, kv_sem.at[2])
    kcopy.start()
    vcopy.start()

    def win_copy(i):
        rows = pl.ds(pl.multiple_of(i * blk, blk), blk)
        return pltpu.make_async_copy(win_hbm.at[0, rows, :], winbuf.at[i], win_sem.at[i])

    def wout_copy(i):
        cols = pl.ds(pl.multiple_of(i * blk, blk), blk)
        return pltpu.make_async_copy(
            wout_hbm.at[0, :, cols], woutbuf.at[lax.rem(i, slots)], wout_sem.at[i]
        )

    @pl.loop(0, BLOCKS)
    def _(i):
        win_copy(i).start()

    wrcopy.start()

    @pl.loop(0, slots)
    def _(i):
        wout_copy(i).start()

    lenbuf[quarter] = jnp.broadcast_to(len_ref[...], lenbuf.shape[1:])
    pl.semaphore_wait(barrier, chips + 1)

    def len_copy(offset):
        peer = lax.rem(quarter + offset, 4)
        return remote(
            lenbuf.at[quarter],
            lenbuf.at[quarter],
            len_send.at[offset],
            len_recv.at[offset],
            base + peer,
        )

    for offset in range(1, 4):
        len_copy(offset).start()

    groups, span = kbuf.shape[1], kbuf.shape[3]
    wide = groups * span
    micros, kv_heads = kbuf.shape[0], kbuf.shape[2]
    per_kv = q_ref.shape[3] // (kv_heads * HD)
    kcopy.wait()
    scores = []
    for m in range(micros):
        query = q_ref[m, 0].astype(F32)
        for h in range(kv_heads):
            rows = jnp.concatenate(
                [
                    query[:, (h * per_kv + j) * HD : (h * per_kv + j + 1) * HD]
                    for j in range(per_kv)
                ],
                axis=0,
            ).astype(BF16)
            keys = kbuf[m, :, h].reshape(wide, HD)
            scores.append(
                lax.dot_general(rows, keys, (((1,), (1,)), ((), ())), preferred_element_type=F32)
                * (1.0 / math.sqrt(HD))
            )
    for offset in range(1, 4):
        len_copy(offset).wait()
    vcopy.wait()
    row_of = lax.broadcasted_iota(jnp.int32, (per_kv * groups, wide), 0) & (groups - 1)
    column = lax.broadcasted_iota(jnp.int32, (per_kv * groups, wide), 1)
    own = row_of == lax.shift_right_logical(column, int(math.log2(span)))
    position = column & (span - 1)
    for m in range(micros):
        used = jnp.concatenate([lenbuf[i, m : m + 1, :] for i in range(groups)], axis=1)
        valid = jnp.logical_and(own, position < used)
        for h in range(kv_heads):
            masked = jnp.where(valid, scores[m * kv_heads + h], -1e30)
            top = jnp.max(masked, axis=-1, keepdims=True)
            expo = jnp.where(valid, jnp.exp(masked - top), 0.0)
            probs = (expo / jnp.sum(expo, axis=-1, keepdims=True)).astype(BF16)
            vals = vbuf[m, :, h].reshape(wide, HD)
            ctx = jnp.dot(probs, vals, preferred_element_type=F32).astype(BF16).astype(F32)
            flat = jnp.concatenate(
                [ctx[j * groups : (j + 1) * groups] for j in range(per_kv)], axis=1
            )
            for i in range(groups):
                ctx_out[i, m * kv_heads + h : m * kv_heads + h + 1, :] = flat[i : i + 1]

    def ctx_copy(offset):
        peer = lax.rem(quarter + offset, 4)
        return remote(
            ctx_out.at[peer],
            ctx_in.at[quarter],
            ctx_send.at[offset],
            ctx_recv.at[offset],
            base + peer,
        )

    for offset in range(1, 4):
        ctx_copy(offset).start()
    ctx_in[quarter] = ctx_out[quarter]
    residual = jnp.concatenate(
        [
            res_ref[m].astype(F32)[:, b * blk : (b + 1) * blk]
            for m in range(micros)
            for b in range(BLOCKS)
        ],
        axis=0,
    )
    for offset in range(1, 4):
        ctx_copy(offset).wait()
    context = jnp.concatenate(
        [
            ctx_in[s, m * kv_heads : (m + 1) * kv_heads, :]
            for m in range(micros)
            for s in range(groups)
        ],
        axis=0,
    )
    state = residual + context
    gain = gain_ref[...]
    pieces = []
    for m in range(micros):
        part = state[m * BLOCKS : (m + 1) * BLOCKS]
        total = jnp.sum(jnp.sum(part * part, axis=1, keepdims=True), axis=0, keepdims=True)
        pieces.append(part * lax.rsqrt(total / (BLOCKS * blk) + 1e-05) * gain)
    normed = jnp.concatenate(pieces, axis=0).astype(BF16)
    gath[me] = normed

    def ag_copy(offset):
        return remote(
            gath.at[me], gath.at[me], ag_send.at[offset], ag_recv.at[offset], same_core(offset)
        )

    def fw_copy(offset):
        source = same_core(chips - offset)
        return remote(
            gath.at[source], gath.at[source], fw_send.at[offset], fw_recv.at[offset], sibling
        )

    @pl.loop(1, chips)
    def _(offset):
        ag_copy(offset).start()

    fw_copy(0).start()

    wrcopy.wait()
    logits = jnp.zeros((micros, EXPERTS), F32)
    for b in range(BLOCKS):
        part = jnp.dot(
            normed, wrbuf[b * blk : (b + 1) * blk, :], preferred_element_type=F32
        )
        logits = logits + jnp.concatenate(
            [part[m * BLOCKS + b : m * BLOCKS + b + 1] for m in range(micros)], axis=0
        )
    gates = jax.nn.sigmoid(logits)
    expert = lax.broadcasted_iota(jnp.int32, (micros, EXPERTS), 1)
    routes = jnp.concatenate([routes_ref[m] for m in range(micros)], axis=0)
    chosen = jnp.zeros((micros, EXPERTS), F32)
    for t in range(routes.shape[1]):
        chosen = chosen + jnp.where(routes[:, t : t + 1] == expert, 1.0, 0.0)
    gates = gates * chosen
    mix = gates / jnp.sum(gates, axis=1, keepdims=True)

    @pl.loop(1, chips)
    def _(offset):
        ag_copy(offset).wait_recv()
        fw_copy(offset).start()

    r = lax.broadcasted_iota(jnp.int32, (256, 256), 0)
    source_row = (((r & 15) >> 1) * 2 + ((r >> 4) & 1)) * 16 + (r & 1) * 8 + (r >> 5)
    order = jnp.where(
        lax.broadcasted_iota(jnp.int32, (256, 256), 1) == source_row, 1.0, 0.0
    ).astype(BF16)

    @pl.loop(0, chips)
    def _(offset):
        fw_copy(offset).wait_recv()

    for g in range(width // 16):
        block = gath[g * 16 : (g + 1) * 16].reshape(256, blk)
        sorted_rows = jnp.dot(order, block, preferred_element_type=F32).astype(BF16)
        for b in range(BLOCKS):
            for c in range(2):
                xbuf[b, c * half + g * 16 : c * half + (g + 1) * 16, :] = sorted_rows[
                    b * 32 + c * 16 : b * 32 + (c + 1) * 16
                ]

    hacc[...] = jnp.zeros_like(hacc)

    @pl.loop(0, BLOCKS)
    def _(i):
        win_copy(i).wait()
        hacc[...] += jnp.dot(xbuf[i], winbuf[i], preferred_element_type=F32)

    pre = hacc[...]
    hid[...] = (pre / (1.0 + jnp.exp(-pre))).astype(BF16)

    def pair_copy(i):
        return remote(pout.at[i], pin.at[i], pair_send.at[i], pair_recv.at[i], sibling)

    def ret_copy(offset, i):
        target = lax.rem(chip + offset, chips)
        return remote(
            rbuf.at[target, i],
            rin.at[chip, i],
            ret_send.at[offset],
            ret_recv.at[offset],
            target * 2 + core,
        )

    def give_back(i):
        pair_copy(i).wait_recv()
        summed = ykeep[lax.rem(i, 2)] + pin[i].astype(F32)
        for t in range(chips):
            rbuf[t, i] = summed[2 * t : 2 * t + 2].astype(BF16)

        @pl.loop(1, chips)
        def _(offset):
            ret_copy(offset, i).start()

        rin[chip, i] = rbuf[chip, i]

    @pl.loop(0, BLOCKS)
    def _(i):
        wout_copy(i).wait()
        part = jnp.dot(hid[...], woutbuf[lax.rem(i, slots)], preferred_element_type=F32)

        @pl.when(i + slots < BLOCKS)
        def _():
            wout_copy(i + slots).start()

        first, second = part[:half], part[half:]
        ykeep[lax.rem(i, 2)] = jnp.where(core == 0, first, second)
        pout[i] = jnp.where(core == 0, second, first).astype(BF16)
        pair_copy(i).start()

        @pl.when(i >= 1)
        def _():
            give_back(i - 1)

    give_back(BLOCKS - 1)

    @pl.loop(1, chips)
    def _(offset):
        ag_copy(offset).wait_send()

    @pl.loop(0, chips)
    def _(offset):
        fw_copy(offset).wait_send()

    @pl.loop(0, BLOCKS)
    def _(i):
        pair_copy(i).wait_send()

    @pl.loop(1, chips)
    def _(offset):
        target = lax.rem(chip + offset, chips)
        source = lax.rem(chip + chips - offset, chips)
        whole = remote(
            rbuf.at[target], rin.at[source], ret_send.at[offset], ret_recv.at[offset], sibling
        )
        whole.wait_send()
        whole.wait_recv()

    split = chips // EXPERTS
    for b in range(BLOCKS):
        total = jnp.concatenate(
            [state[m * BLOCKS + b : m * BLOCKS + b + 1] for m in range(micros)], axis=0
        )
        for x in range(EXPERTS):
            out_x = rin[x * split, b].astype(F32)
            for s in range(1, split):
                out_x = out_x + rin[x * split + s, b].astype(F32)
            total = total + mix[:, x : x + 1] * out_x
        total = total.astype(BF16)
        for m in range(micros):
            out_ref[m, :, b * blk : (b + 1) * blk] = total[m : m + 1]


def on_device(queries, keys, values, lengths, routes, residual, gain, w_router, w_in, w_out):
    width = lax.axis_size("ex")
    chips = width // 2
    micros = queries.shape[0]
    rows = micros * width
    hidden = w_in.shape[2]
    model = residual.shape[2]
    blk = model // BLOCKS
    dma = pltpu.SemaphoreType.DMA
    vmem = pltpu.VMEM
    in_vmem = pl.BlockSpec(memory_space=pltpu.VMEM)
    anywhere = pl.BlockSpec(memory_space=pl.ANY)
    return pl.pallas_call(
        functools.partial(layer_kernel, width),
        out_shape=jax.ShapeDtypeStruct(residual.shape, BF16),
        in_specs=[in_vmem] * 5 + [anywhere] * 5,
        out_specs=in_vmem,
        scratch_shapes=[
            vmem((micros,) + keys.shape[2:], BF16),
            vmem((micros,) + values.shape[2:], BF16),
            vmem(w_router.shape, BF16),
            vmem((BLOCKS, blk, hidden), BF16),
            vmem((OUT_SLOTS, hidden, blk), BF16),
            vmem((4, micros, keys.shape[4]), jnp.int32),
            vmem((4, 4, blk), F32),
            vmem((4, 4, blk), F32),
            vmem((width, 16, blk), BF16),
            vmem((BLOCKS, rows, blk), BF16),
            vmem((rows, hidden), F32),
            vmem((rows, hidden), BF16),
            vmem((2, rows // 2, blk), F32),
            vmem((BLOCKS, rows // 2, blk), BF16),
            vmem((BLOCKS, rows // 2, blk), BF16),
            vmem((chips, BLOCKS, 2, blk), BF16),
            vmem((chips, BLOCKS, 2, blk), BF16),
            dma((3,)),
            dma((BLOCKS,)),
            dma((BLOCKS,)),
            dma((4,)),
            dma((4,)),
            dma((4,)),
            dma((4,)),
            dma((chips,)),
            dma((chips,)),
            dma((chips,)),
            dma((chips,)),
            dma((BLOCKS,)),
            dma((BLOCKS,)),
            dma((chips,)),
            dma((chips,)),
        ],
        compiler_params=pltpu.CompilerParams(
            collective_id=0, has_side_effects=True, vmem_limit_bytes=61 * 1024 * 1024
        ),
    )(
        queries,
        lengths,
        routes,
        residual,
        gain.reshape(BLOCKS, blk).astype(F32),
        keys.reshape((micros,) + keys.shape[2:]),
        values.reshape((micros,) + values.shape[2:]),
        w_router,
        w_in,
        w_out,
    )


def solution(mesh):
    return jax.shard_map(
        on_device,
        mesh=mesh,
        in_specs=(
            P(None, ("grp", "ex"), None, None),
            P(None, ("grp", "ex"), None, None, None, None),
            P(None, ("grp", "ex"), None, None, None, None),
            P(None, ("grp", "ex")),
            P(None, ("grp", "ex"), None),
            P(None, ("grp", "ex"), None),
            P(),
            P(),
            P("ex", None, None),
            P("ex", None, None),
        ),
        out_specs=P(None, ("grp", "ex"), None),
        check_vma=False,
    )
```

```python
import functools
import math

import jax
import jax.numpy as jnp
from jax import lax
from jax.experimental import pallas as pl
from jax.experimental.pallas import tpu as pltpu
from jax.sharding import PartitionSpec as P

HD = 128
EXPERTS = 8
BLOCKS = 6
GROUPS = 3
PIECES = 8
OUT_SLOTS = 4
F32 = jnp.float32
BF16 = jnp.bfloat16


def layer_kernel(
    width,
    q_ref,
    len_ref,
    routes_ref,
    res_ref,
    gain_ref,
    k_hbm,
    v_hbm,
    wr_hbm,
    win_hbm,
    wout_hbm,
    out_ref,
    kbuf,
    vbuf,
    wrbuf,
    winbuf,
    woutbuf,
    lenbuf,
    ctx_out,
    ctx_in,
    gath,
    xbuf,
    hacc,
    hid,
    ykeep,
    pout,
    pin,
    rbuf,
    rin,
    kv_sem,
    win_sem,
    wout_sem,
    len_send,
    len_recv,
    ctx_send,
    ctx_recv,
    ag_send,
    ag_recv,
    fw_send,
    fw_recv,
    pair_send,
    pair_recv,
    ret_send,
    ret_recv,
):
    me = lax.axis_index("ex")
    chips = width // 2
    chip = me // 2
    core = me % 2
    quarter = me % 4
    base = me - quarter
    sibling = me + 1 - 2 * core
    blk = gain_ref.shape[0] * gain_ref.shape[1] // BLOCKS
    piece = blk * BLOCKS // (GROUPS * PIECES)
    per_blk = blk // piece
    blk_group = BLOCKS // GROUPS
    half = width
    slots = woutbuf.shape[0]

    def same_core(offset):
        return lax.rem(chip + offset, chips) * 2 + core

    def remote(src, dst, send, recv, target):
        return pltpu.make_async_remote_copy(
            src_ref=src,
            dst_ref=dst,
            send_sem=send,
            recv_sem=recv,
            device_id={"ex": target},
            device_id_type=pl.DeviceIdType.MESH,
        )

    barrier = pltpu.get_barrier_semaphore()
    diagonal = base + 3 - quarter

    def greet(device):
        pl.semaphore_signal(
            barrier, inc=1, device_id={"ex": device}, device_id_type=pl.DeviceIdType.MESH
        )

    @pl.loop(1, chips)
    def _(offset):
        greet(same_core(offset))

    greet(sibling)
    greet(diagonal)

    kcopy = pltpu.make_async_copy(k_hbm, kbuf, kv_sem.at[0])
    vcopy = pltpu.make_async_copy(v_hbm, vbuf, kv_sem.at[1])
    wrcopy = pltpu.make_async_copy(wr_hbm, wrbuf, kv_sem.at[2])
    kcopy.start()
    vcopy.start()

    def win_copy(i):
        rows = pl.ds(pl.multiple_of(i * blk, blk), blk)
        return pltpu.make_async_copy(win_hbm.at[0, rows, :], winbuf.at[i], win_sem.at[i])

    def wout_copy(i):
        cols = pl.ds(pl.multiple_of(i * blk, blk), blk)
        return pltpu.make_async_copy(
            wout_hbm.at[0, :, cols], woutbuf.at[lax.rem(i, slots)], wout_sem.at[i]
        )

    @pl.loop(0, BLOCKS)
    def _(i):
        win_copy(i).start()

    wrcopy.start()

    @pl.loop(0, slots)
    def _(i):
        wout_copy(i).start()

    for m in range(lenbuf.shape[1]):
        lenbuf[quarter, m : m + 1, :] = jnp.broadcast_to(
            len_ref[:, m : m + 1], (1, lenbuf.shape[2])
        )
    pl.semaphore_wait(barrier, chips + 1)

    def len_copy(offset):
        peer = lax.rem(quarter + offset, 4)
        return remote(
            lenbuf.at[quarter],
            lenbuf.at[quarter],
            len_send.at[offset],
            len_recv.at[offset],
            base + peer,
        )

    for offset in range(1, 4):
        len_copy(offset).start()

    groups, span = kbuf.shape[1], kbuf.shape[3]
    wide = groups * span
    micros, kv_heads = kbuf.shape[0], kbuf.shape[2]
    per_kv = q_ref.shape[3] // (kv_heads * HD)
    kcopy.wait()
    scores = []
    for m in range(micros):
        query = q_ref[m, 0].astype(F32)
        for h in range(kv_heads):
            rows = jnp.concatenate(
                [
                    query[:, (h * per_kv + j) * HD : (h * per_kv + j + 1) * HD]
                    for j in range(per_kv)
                ],
                axis=0,
            ).astype(BF16)
            keys = kbuf[m, :, h].reshape(wide, HD)
            scores.append(
                lax.dot_general(rows, keys, (((1,), (1,)), ((), ())), preferred_element_type=F32)
                * (1.0 / math.sqrt(HD))
            )
    for offset in range(1, 4):
        len_copy(offset).wait()
    vcopy.wait()
    row_of = lax.broadcasted_iota(jnp.int32, (per_kv * groups, wide), 0) & (groups - 1)
    column = lax.broadcasted_iota(jnp.int32, (per_kv * groups, wide), 1)
    own = row_of == lax.shift_right_logical(column, int(math.log2(span)))
    position = column & (span - 1)
    for m in range(micros):
        used = jnp.concatenate([lenbuf[i, m : m + 1, :] for i in range(groups)], axis=1)
        valid = jnp.logical_and(own, position < used)
        for h in range(kv_heads):
            masked = jnp.where(valid, scores[m * kv_heads + h], -1e30)
            top = jnp.max(masked, axis=-1, keepdims=True)
            expo = jnp.where(valid, jnp.exp(masked - top), 0.0)
            probs = (expo / jnp.sum(expo, axis=-1, keepdims=True)).astype(BF16)
            vals = vbuf[m, :, h].reshape(wide, HD)
            ctx = jnp.dot(probs, vals, preferred_element_type=F32).astype(BF16).astype(F32)
            flat = jnp.concatenate(
                [ctx[j * groups : (j + 1) * groups] for j in range(per_kv)], axis=1
            )
            for i in range(groups):
                ctx_out[i, m * kv_heads + h : m * kv_heads + h + 1, :] = flat[i : i + 1]

    def ctx_copy(offset):
        peer = lax.rem(quarter + offset, 4)
        return remote(
            ctx_out.at[peer],
            ctx_in.at[quarter],
            ctx_send.at[offset],
            ctx_recv.at[offset],
            base + peer,
        )

    for offset in range(1, 4):
        ctx_copy(offset).start()
    ctx_in[quarter] = ctx_out[quarter]
    residual = res_ref[...].astype(F32)
    gain_rows = gain_ref[...].astype(F32)
    lanes = piece // HD

    def by_piece(take, g):
        return jnp.concatenate(
            [take(m, g * PIECES + k) for m in range(micros) for k in range(PIECES)], axis=0
        )

    res_parts = [
        by_piece(lambda m, p: residual[m : m + 1, p * piece : (p + 1) * piece], g)
        for g in range(GROUPS)
    ]
    gains = [
        by_piece(
            lambda m, p: jnp.concatenate(
                [gain_rows[p * lanes + t : p * lanes + t + 1] for t in range(lanes)], axis=1
            ),
            g,
        )
        for g in range(GROUPS)
    ]
    for offset in range(1, 4):
        ctx_copy(offset).wait()
    context = ctx_in[...]
    head_pieces = ctx_in.shape[2] // piece

    def ctx_piece(m, p):
        head, t = p // head_pieces, p % head_pieces
        row = m * kv_heads + head % kv_heads
        return context[head // kv_heads, row : row + 1, t * piece : (t + 1) * piece]

    state = [res_parts[g] + by_piece(ctx_piece, g) for g in range(GROUPS)]
    squares = sum(jnp.sum(part * part, axis=1, keepdims=True) for part in state)
    scale = jnp.concatenate(
        [
            jnp.broadcast_to(
                lax.rsqrt(
                    jnp.sum(squares[m * PIECES : (m + 1) * PIECES], axis=0, keepdims=True)
                    / (BLOCKS * blk)
                    + 1e-05
                ),
                (PIECES, 1),
            )
            for m in range(micros)
        ],
        axis=0,
    )
    normed = [(state[g] * scale * gains[g]).astype(BF16) for g in range(GROUPS)]
    for g in range(GROUPS):
        gath[me, g] = normed[g]

    parts = (pl.ds(0, 1), pl.ds(1, GROUPS - 1))

    def ag_copy(offset, p):
        own_part = gath.at[me, parts[p]]
        return remote(
            own_part, own_part, ag_send.at[p, offset], ag_recv.at[p, offset], same_core(offset)
        )

    def fw_copy(offset, p):
        part = gath.at[same_core(chips - offset), parts[p]]
        return remote(part, part, fw_send.at[p, offset], fw_recv.at[p, offset], sibling)

    for p in range(2):

        @pl.loop(1, chips)
        def _(offset):
            ag_copy(offset, p).start()

        fw_copy(0, p).start()

    wrcopy.wait()
    logits = jnp.zeros((micros, EXPERTS), F32)
    for p in range(GROUPS * PIECES):
        part = lax.dot_general(
            normed[p // PIECES],
            wrbuf[:, p * piece : (p + 1) * piece],
            (((1,), (1,)), ((), ())),
            preferred_element_type=F32,
        )
        k = p % PIECES
        logits = logits + jnp.concatenate(
            [part[m * PIECES + k : m * PIECES + k + 1] for m in range(micros)], axis=0
        )
    gates = jax.nn.sigmoid(logits)
    expert = lax.broadcasted_iota(jnp.int32, (micros, EXPERTS), 1)
    routes = jnp.concatenate([routes_ref[m] for m in range(micros)], axis=0)
    chosen = jnp.zeros((micros, EXPERTS), F32)
    for t in range(routes.shape[1]):
        chosen = chosen + jnp.where(routes[:, t : t + 1] == expert, 1.0, 0.0)
    gates = gates * chosen
    mix = gates / jnp.sum(gates, axis=1, keepdims=True)

    mix_rows = jnp.concatenate(
        [jnp.broadcast_to(mix[m : m + 1], (PIECES, EXPERTS)) for m in range(micros)], axis=0
    )

    r = lax.broadcasted_iota(jnp.int32, (256, 256), 0)
    source_row = (((r & 15) >> 1) * 2 + ((r >> 4) & 1)) * 16 + (r & 1) * 8 + (r >> 5)
    order = jnp.where(
        lax.broadcasted_iota(jnp.int32, (256, 256), 1) == source_row, 1.0, 0.0
    ).astype(BF16)
    r = lax.broadcasted_iota(jnp.int32, (128, 128), 0)
    source_row = (r & 7) * 16 + (r >> 4) * 2 + ((r >> 3) & 1)
    order_back = jnp.where(
        lax.broadcasted_iota(jnp.int32, (128, 128), 1) == source_row, 1.0, 0.0
    ).astype(BF16)

    def forward(p):
        @pl.loop(1, chips)
        def _(offset):
            ag_copy(offset, p).wait_recv()
            fw_copy(offset, p).start()

    def arrived(p):
        @pl.loop(0, chips)
        def _(offset):
            fw_copy(offset, p).wait_recv()

    def sort_rows(g):
        for w in range(width // 16):
            block = gath[w * 16 : (w + 1) * 16, g].reshape(256, piece)
            rows = jnp.dot(order, block, preferred_element_type=F32).astype(BF16)
            for k in range(PIECES):
                for c in range(2):
                    xbuf[g * PIECES + k, c * half + w * 16 : c * half + (w + 1) * 16, :] = rows[
                        k * 32 + c * 16 : k * 32 + (c + 1) * 16
                    ]

    def project(i):
        win_copy(i).wait()
        rows = jnp.concatenate([xbuf[i * per_blk + t] for t in range(per_blk)], axis=1)
        hacc[...] += jnp.dot(rows, winbuf[i], preferred_element_type=F32)

    hacc[...] = jnp.zeros_like(hacc)
    forward(0)
    arrived(0)
    sort_rows(0)
    project(0)
    forward(1)
    project(1)
    arrived(1)
    for g in range(1, GROUPS):
        sort_rows(g)

    @pl.loop(blk_group, BLOCKS)
    def _(i):
        project(i)

    pre = hacc[...]
    hid[...] = (pre / (1.0 + jnp.exp(-pre))).astype(BF16)

    def pair_copy(i):
        return remote(pout.at[i], pin.at[i], pair_send.at[i], pair_recv.at[i], sibling)

    def ret_copy(offset, g):
        target = lax.rem(chip + offset, chips)
        return remote(
            rbuf.at[g, target],
            rin.at[g, chip],
            ret_send.at[g, offset],
            ret_recv.at[g, offset],
            target * 2 + core,
        )

    def expand(i):
        wout_copy(i).wait()
        part = jnp.dot(hid[...], woutbuf[lax.rem(i, slots)], preferred_element_type=F32)
        first, second = part[:half], part[half:]
        ykeep[i] = jnp.where(core == 0, first, second)
        pout[i] = jnp.where(core == 0, second, first).astype(BF16)
        pair_copy(i).start()

    def give_back(g):
        blocks = range(g * blk_group, (g + 1) * blk_group)
        for i in blocks:
            pair_copy(i).wait_recv()
        summed = [(ykeep[i] + pin[i].astype(F32)).astype(BF16) for i in blocks]
        for w in range(chips // 8):
            stacked = jnp.concatenate(
                [
                    summed[k // per_blk][
                        w * 16 : (w + 1) * 16,
                        (k % per_blk) * piece : (k % per_blk + 1) * piece,
                    ]
                    for k in range(PIECES)
                ],
                axis=0,
            )
            rows = jnp.dot(order_back, stacked, preferred_element_type=F32).astype(BF16)
            for t in range(8):
                rbuf[g, w * 8 + t] = rows[t * 16 : (t + 1) * 16]

        @pl.loop(1, chips)
        def _(offset):
            ret_copy(offset, g).start()

        rin[g, chip] = rbuf[g, chip]

    for i in range(BLOCKS):
        expand(i)
        if i + slots < BLOCKS:
            wout_copy(i + slots).start()
        if i >= blk_group and i % blk_group == 0:
            give_back(i // blk_group - 1)
    give_back(GROUPS - 1)

    @pl.loop(1, chips)
    def _(offset):
        for p in range(2):
            ag_copy(offset, p).wait_send()
            fw_copy(offset, p).wait_send()

    for p in range(2):
        fw_copy(0, p).wait_send()

    @pl.loop(0, BLOCKS)
    def _(i):
        pair_copy(i).wait_send()

    split = chips // EXPERTS
    for g in range(GROUPS):

        @pl.loop(1, chips)
        def _(offset):
            ret_copy(offset, g).wait()

        total = state[g]
        for x in range(EXPERTS):
            out_x = rin[g, x * split].astype(F32)
            for t in range(1, split):
                out_x = out_x + rin[g, x * split + t].astype(F32)
            total = total + mix_rows[:, x : x + 1] * out_x
        flat = jnp.concatenate(
            [
                jnp.concatenate(
                    [total[m * PIECES + k : m * PIECES + k + 1] for m in range(micros)], axis=0
                )
                for k in range(PIECES)
            ],
            axis=1,
        )
        out_ref[:, g * PIECES * piece : (g + 1) * PIECES * piece] = flat.astype(BF16)


def on_device(queries, keys, values, lengths, routes, residual, gain, w_router, w_in, w_out):
    width = lax.axis_size("ex")
    chips = width // 2
    micros = queries.shape[0]
    rows = micros * width
    hidden = w_in.shape[2]
    model = residual.shape[2]
    blk = model // BLOCKS
    piece = model // (GROUPS * PIECES)
    head = queries.shape[3] // keys.shape[3]
    dma = pltpu.SemaphoreType.DMA
    vmem = pltpu.VMEM
    in_vmem = pl.BlockSpec(memory_space=pltpu.VMEM)
    anywhere = pl.BlockSpec(memory_space=pl.ANY)
    return pl.pallas_call(
        functools.partial(layer_kernel, width),
        out_shape=jax.ShapeDtypeStruct((micros, model), BF16),
        in_specs=[in_vmem] * 5 + [anywhere] * 5,
        out_specs=in_vmem,
        scratch_shapes=[
            vmem((micros,) + keys.shape[2:], BF16),
            vmem((micros,) + values.shape[2:], BF16),
            vmem(w_router.shape[::-1], BF16),
            vmem((BLOCKS, blk, hidden), BF16),
            vmem((OUT_SLOTS, hidden, blk), BF16),
            vmem((4, micros, keys.shape[4]), jnp.int32),
            vmem((4, 4, head), F32),
            vmem((4, 4, head), F32),
            vmem((width, GROUPS, 16, piece), BF16),
            vmem((GROUPS * PIECES, rows, piece), BF16),
            vmem((rows, hidden), F32),
            vmem((rows, hidden), BF16),
            vmem((BLOCKS, rows // 2, blk), F32),
            vmem((BLOCKS, rows // 2, blk), BF16),
            vmem((BLOCKS, rows // 2, blk), BF16),
            vmem((GROUPS, chips, 16, piece), BF16),
            vmem((GROUPS, chips, 16, piece), BF16),
            dma((3,)),
            dma((BLOCKS,)),
            dma((BLOCKS,)),
            dma((4,)),
            dma((4,)),
            dma((4,)),
            dma((4,)),
            dma((2, chips)),
            dma((2, chips)),
            dma((2, chips)),
            dma((2, chips)),
            dma((BLOCKS,)),
            dma((BLOCKS,)),
            dma((GROUPS, chips)),
            dma((GROUPS, chips)),
        ],
        compiler_params=pltpu.CompilerParams(
            collective_id=0, has_side_effects=True, vmem_limit_bytes=61 * 1024 * 1024
        ),
    )(
        queries,
        lengths.T,
        routes,
        residual.reshape(micros, model),
        gain.reshape(model // HD, HD),
        keys.reshape((micros,) + keys.shape[2:]),
        values.reshape((micros,) + values.shape[2:]),
        w_router.T,
        w_in,
        w_out,
    ).reshape(residual.shape)


def solution(mesh):
    return jax.shard_map(
        on_device,
        mesh=mesh,
        in_specs=(
            P(None, ("grp", "ex"), None, None),
            P(None, ("grp", "ex"), None, None, None, None),
            P(None, ("grp", "ex"), None, None, None, None),
            P(None, ("grp", "ex")),
            P(None, ("grp", "ex"), None),
            P(None, ("grp", "ex"), None),
            P(),
            P(),
            P("ex", None, None),
            P("ex", None, None),
        ),
        out_specs=P(None, ("grp", "ex"), None),
        check_vma=False,
    )
```

```python
import functools
import math

import jax
import jax.numpy as jnp
from jax import lax
from jax.experimental import pallas as pl
from jax.experimental.pallas import tpu as pltpu
from jax.sharding import PartitionSpec as P

HD = 128
EXPERTS = 8
BLOCKS = 6
GROUPS = 3
PIECES = 8
OUT_SLOTS = 4
F32 = jnp.float32
BF16 = jnp.bfloat16


def layer_kernel(
    width,
    q_ref,
    len_ref,
    routes_ref,
    res_ref,
    gain_ref,
    k_hbm,
    v_hbm,
    wr_hbm,
    win_hbm,
    wout_hbm,
    out_ref,
    kbuf,
    vbuf,
    wrbuf,
    winbuf,
    woutbuf,
    lenbuf,
    ctx_out,
    ctx_in,
    gath,
    xbuf,
    hacc,
    hid,
    ykeep,
    pout,
    pin,
    rbuf,
    rin,
    kv_sem,
    win_sem,
    wout_sem,
    len_send,
    len_recv,
    ctx_send,
    ctx_recv,
    ag_send,
    ag_recv,
    fw_send,
    fw_recv,
    pair_send,
    pair_recv,
    ret_send,
    ret_recv,
):
    me = lax.axis_index("ex")
    chips = width // 2
    chip = me // 2
    core = me % 2
    quarter = me % 4
    base = me - quarter
    sibling = me + 1 - 2 * core
    blk = gain_ref.shape[0] * gain_ref.shape[1] // BLOCKS
    piece = blk * BLOCKS // (GROUPS * PIECES)
    per_blk = blk // piece
    blk_group = BLOCKS // GROUPS
    half = width
    slots = woutbuf.shape[0]

    def same_core(offset):
        return lax.rem(chip + offset, chips) * 2 + core

    def remote(src, dst, send, recv, target):
        return pltpu.make_async_remote_copy(
            src_ref=src,
            dst_ref=dst,
            send_sem=send,
            recv_sem=recv,
            device_id={"ex": target},
            device_id_type=pl.DeviceIdType.MESH,
        )

    barrier = pltpu.get_barrier_semaphore()
    diagonal = base + 3 - quarter

    def greet(device):
        pl.semaphore_signal(
            barrier, inc=1, device_id={"ex": device}, device_id_type=pl.DeviceIdType.MESH
        )

    @pl.loop(1, chips)
    def _(offset):
        greet(same_core(offset))

    greet(sibling)
    greet(diagonal)

    kcopy = pltpu.make_async_copy(k_hbm, kbuf, kv_sem.at[0])
    vcopy = pltpu.make_async_copy(v_hbm, vbuf, kv_sem.at[1])
    wrcopy = pltpu.make_async_copy(wr_hbm, wrbuf, kv_sem.at[2])
    kcopy.start()
    vcopy.start()

    def win_copy(i):
        rows = pl.ds(pl.multiple_of(i * blk, blk), blk)
        return pltpu.make_async_copy(win_hbm.at[0, rows, :], winbuf.at[i], win_sem.at[i])

    def wout_copy(i):
        cols = pl.ds(pl.multiple_of(i * blk, blk), blk)
        return pltpu.make_async_copy(
            wout_hbm.at[0, :, cols], woutbuf.at[lax.rem(i, slots)], wout_sem.at[i]
        )

    @pl.loop(0, BLOCKS)
    def _(i):
        win_copy(i).start()

    for m in range(lenbuf.shape[1]):
        lenbuf[quarter, m : m + 1, :] = jnp.broadcast_to(
            len_ref[:, m : m + 1], (1, lenbuf.shape[2])
        )
    pl.semaphore_wait(barrier, chips + 1)

    def len_copy(offset):
        peer = lax.rem(quarter + offset, 4)
        return remote(
            lenbuf.at[quarter],
            lenbuf.at[quarter],
            len_send.at[offset],
            len_recv.at[offset],
            base + peer,
        )

    for offset in range(1, 4):
        len_copy(offset).start()

    wrcopy.start()

    @pl.loop(0, slots)
    def _(i):
        wout_copy(i).start()

    groups, span = kbuf.shape[1], kbuf.shape[3]
    wide = groups * span
    micros, kv_heads = kbuf.shape[0], kbuf.shape[2]
    per_kv = q_ref.shape[3] // (kv_heads * HD)
    kcopy.wait()
    scores = []
    for m in range(micros):
        query = q_ref[m, 0].astype(F32)
        for h in range(kv_heads):
            rows = jnp.concatenate(
                [
                    query[:, (h * per_kv + j) * HD : (h * per_kv + j + 1) * HD]
                    for j in range(per_kv)
                ],
                axis=0,
            ).astype(BF16)
            keys = kbuf[m, :, h].reshape(wide, HD)
            scores.append(
                lax.dot_general(rows, keys, (((1,), (1,)), ((), ())), preferred_element_type=F32)
                * (1.0 / math.sqrt(HD))
            )
    for offset in range(1, 4):
        len_copy(offset).wait()
    vcopy.wait()
    row_of = lax.broadcasted_iota(jnp.int32, (per_kv * groups, wide), 0) & (groups - 1)
    column = lax.broadcasted_iota(jnp.int32, (per_kv * groups, wide), 1)
    own = row_of == lax.shift_right_logical(column, int(math.log2(span)))
    position = column & (span - 1)
    for m in range(micros):
        used = jnp.concatenate([lenbuf[i, m : m + 1, :] for i in range(groups)], axis=1)
        valid = jnp.logical_and(own, position < used)
        for h in range(kv_heads):
            masked = jnp.where(valid, scores[m * kv_heads + h], -1e30)
            top = jnp.max(masked, axis=-1, keepdims=True)
            expo = jnp.where(valid, jnp.exp(masked - top), 0.0)
            probs = (expo / jnp.sum(expo, axis=-1, keepdims=True)).astype(BF16)
            vals = vbuf[m, :, h].reshape(wide, HD)
            ctx = jnp.dot(probs, vals, preferred_element_type=F32).astype(BF16).astype(F32)
            flat = jnp.concatenate(
                [ctx[j * groups : (j + 1) * groups] for j in range(per_kv)], axis=1
            )
            for i in range(groups):
                ctx_out[i, m * kv_heads + h : m * kv_heads + h + 1, :] = flat[i : i + 1]

    def ctx_copy(offset):
        peer = lax.rem(quarter + offset, 4)
        return remote(
            ctx_out.at[peer],
            ctx_in.at[quarter],
            ctx_send.at[offset],
            ctx_recv.at[offset],
            base + peer,
        )

    for offset in range(1, 4):
        ctx_copy(offset).start()
    ctx_in[quarter] = ctx_out[quarter]
    residual = res_ref[...].astype(F32)
    gain_rows = gain_ref[...].astype(F32)
    lanes = piece // HD

    def by_piece(take, g):
        return jnp.concatenate(
            [take(m, g * PIECES + k) for m in range(micros) for k in range(PIECES)], axis=0
        )

    res_parts = [
        by_piece(lambda m, p: residual[m : m + 1, p * piece : (p + 1) * piece], g)
        for g in range(GROUPS)
    ]
    gains = [
        by_piece(
            lambda m, p: jnp.concatenate(
                [gain_rows[p * lanes + t : p * lanes + t + 1] for t in range(lanes)], axis=1
            ),
            g,
        )
        for g in range(GROUPS)
    ]
    for offset in range(1, 4):
        ctx_copy(offset).wait()
    context = ctx_in[...]
    head_pieces = ctx_in.shape[2] // piece

    def ctx_piece(m, p):
        head, t = p // head_pieces, p % head_pieces
        row = m * kv_heads + head % kv_heads
        return context[head // kv_heads, row : row + 1, t * piece : (t + 1) * piece]

    state = [res_parts[g] + by_piece(ctx_piece, g) for g in range(GROUPS)]
    squares = sum(jnp.sum(part * part, axis=1, keepdims=True) for part in state)
    scale = jnp.concatenate(
        [
            jnp.broadcast_to(
                lax.rsqrt(
                    jnp.sum(squares[m * PIECES : (m + 1) * PIECES], axis=0, keepdims=True)
                    / (BLOCKS * blk)
                    + 1e-05
                ),
                (PIECES, 1),
            )
            for m in range(micros)
        ],
        axis=0,
    )
    normed = [(state[g] * scale * gains[g]).astype(BF16) for g in range(GROUPS)]
    for g in range(GROUPS):
        gath[me, g] = normed[g]

    parts = (pl.ds(0, 1), pl.ds(1, GROUPS - 1))

    def ag_copy(offset, p):
        own_part = gath.at[me, parts[p]]
        return remote(
            own_part, own_part, ag_send.at[p, offset], ag_recv.at[p, offset], same_core(offset)
        )

    def fw_copy(offset, p):
        part = gath.at[same_core(chips - offset), parts[p]]
        return remote(part, part, fw_send.at[p, offset], fw_recv.at[p, offset], sibling)

    for p in range(2):

        @pl.loop(1, chips)
        def _(offset):
            ag_copy(offset, p).start()

        fw_copy(0, p).start()

    r = lax.broadcasted_iota(jnp.int32, (256, 256), 0)
    source_row = (((r & 15) >> 1) * 2 + ((r >> 4) & 1)) * 16 + (r & 1) * 8 + (r >> 5)
    order = jnp.where(
        lax.broadcasted_iota(jnp.int32, (256, 256), 1) == source_row, 1.0, 0.0
    ).astype(BF16)
    r = lax.broadcasted_iota(jnp.int32, (128, 128), 0)
    source_row = (r & 7) * 16 + (r >> 4) * 2 + ((r >> 3) & 1)
    order_back = jnp.where(
        lax.broadcasted_iota(jnp.int32, (128, 128), 1) == source_row, 1.0, 0.0
    ).astype(BF16)

    def forward(p):
        @pl.loop(1, chips)
        def _(offset):
            ag_copy(offset, p).wait_recv()
            fw_copy(offset, p).start()

    def arrived(p):
        @pl.loop(0, chips)
        def _(offset):
            fw_copy(offset, p).wait_recv()

    def sort_rows(g):
        for w in range(width // 16):
            block = gath[w * 16 : (w + 1) * 16, g].reshape(256, piece)
            rows = jnp.dot(order, block, preferred_element_type=F32).astype(BF16)
            for k in range(PIECES):
                for c in range(2):
                    xbuf[g * PIECES + k, c * half + w * 16 : c * half + (w + 1) * 16, :] = rows[
                        k * 32 + c * 16 : k * 32 + (c + 1) * 16
                    ]

    def project(i):
        win_copy(i).wait()
        rows = jnp.concatenate([xbuf[i * per_blk + t] for t in range(per_blk)], axis=1)
        hacc[...] += jnp.dot(rows, winbuf[i], preferred_element_type=F32)

    hacc[...] = jnp.zeros_like(hacc)
    forward(0)
    arrived(0)
    sort_rows(0)
    project(0)
    forward(1)
    project(1)
    arrived(1)
    for g in range(1, GROUPS):
        sort_rows(g)

    @pl.loop(blk_group, BLOCKS)
    def _(i):
        project(i)

    pre = hacc[...]
    hid[...] = (pre / (1.0 + jnp.exp(-pre))).astype(BF16)

    def pair_copy(i):
        return remote(pout.at[i], pin.at[i], pair_send.at[i], pair_recv.at[i], sibling)

    def ret_copy(offset, g):
        target = lax.rem(chip + offset, chips)
        return remote(
            rbuf.at[g, target],
            rin.at[g, chip],
            ret_send.at[g, offset],
            ret_recv.at[g, offset],
            target * 2 + core,
        )

    def expand(i):
        wout_copy(i).wait()
        part = jnp.dot(hid[...], woutbuf[lax.rem(i, slots)], preferred_element_type=F32)
        first, second = part[:half], part[half:]
        ykeep[i] = jnp.where(core == 0, first, second)
        pout[i] = jnp.where(core == 0, second, first).astype(BF16)
        pair_copy(i).start()

    def give_back(g):
        blocks = range(g * blk_group, (g + 1) * blk_group)
        for i in blocks:
            pair_copy(i).wait_recv()
        summed = [(ykeep[i] + pin[i].astype(F32)).astype(BF16) for i in blocks]
        for w in range(chips // 8):
            stacked = jnp.concatenate(
                [
                    summed[k // per_blk][
                        w * 16 : (w + 1) * 16,
                        (k % per_blk) * piece : (k % per_blk + 1) * piece,
                    ]
                    for k in range(PIECES)
                ],
                axis=0,
            )
            rows = jnp.dot(order_back, stacked, preferred_element_type=F32).astype(BF16)
            for t in range(8):
                rbuf[g, w * 8 + t] = rows[t * 16 : (t + 1) * 16]

        @pl.loop(1, chips)
        def _(offset):
            ret_copy(offset, g).start()

        rin[g, chip] = rbuf[g, chip]

    for i in range(BLOCKS):
        expand(i)
        if i + slots < BLOCKS:
            wout_copy(i + slots).start()
        if i >= blk_group and i % blk_group == 0:
            give_back(i // blk_group - 1)
    give_back(GROUPS - 1)

    wrcopy.wait()
    logits = jnp.zeros((micros, EXPERTS), F32)
    for p in range(GROUPS * PIECES):
        part = lax.dot_general(
            normed[p // PIECES],
            wrbuf[:, p * piece : (p + 1) * piece],
            (((1,), (1,)), ((), ())),
            preferred_element_type=F32,
        )
        k = p % PIECES
        logits = logits + jnp.concatenate(
            [part[m * PIECES + k : m * PIECES + k + 1] for m in range(micros)], axis=0
        )
    gates = jax.nn.sigmoid(logits)
    expert = lax.broadcasted_iota(jnp.int32, (micros, EXPERTS), 1)
    routes = jnp.concatenate([routes_ref[m] for m in range(micros)], axis=0)
    chosen = jnp.zeros((micros, EXPERTS), F32)
    for t in range(routes.shape[1]):
        chosen = chosen + jnp.where(routes[:, t : t + 1] == expert, 1.0, 0.0)
    gates = gates * chosen
    mix = gates / jnp.sum(gates, axis=1, keepdims=True)

    mix_rows = jnp.concatenate(
        [jnp.broadcast_to(mix[m : m + 1], (PIECES, EXPERTS)) for m in range(micros)], axis=0
    )

    @pl.loop(1, chips)
    def _(offset):
        for p in range(2):
            ag_copy(offset, p).wait_send()
            fw_copy(offset, p).wait_send()

    for p in range(2):
        fw_copy(0, p).wait_send()

    @pl.loop(0, BLOCKS)
    def _(i):
        pair_copy(i).wait_send()

    split = chips // EXPERTS
    for g in range(GROUPS):

        @pl.loop(1, chips)
        def _(offset):
            ret_copy(offset, g).wait()

        total = state[g]
        for x in range(EXPERTS):
            out_x = rin[g, x * split].astype(F32)
            for t in range(1, split):
                out_x = out_x + rin[g, x * split + t].astype(F32)
            total = total + mix_rows[:, x : x + 1] * out_x
        flat = jnp.concatenate(
            [
                jnp.concatenate(
                    [total[m * PIECES + k : m * PIECES + k + 1] for m in range(micros)], axis=0
                )
                for k in range(PIECES)
            ],
            axis=1,
        )
        out_ref[:, g * PIECES * piece : (g + 1) * PIECES * piece] = flat.astype(BF16)


def on_device(queries, keys, values, lengths, routes, residual, gain, w_router, w_in, w_out):
    width = lax.axis_size("ex")
    chips = width // 2
    micros = queries.shape[0]
    rows = micros * width
    hidden = w_in.shape[2]
    model = residual.shape[2]
    blk = model // BLOCKS
    piece = model // (GROUPS * PIECES)
    head = queries.shape[3] // keys.shape[3]
    dma = pltpu.SemaphoreType.DMA
    vmem = pltpu.VMEM
    in_vmem = pl.BlockSpec(memory_space=pltpu.VMEM)
    anywhere = pl.BlockSpec(memory_space=pl.ANY)
    return pl.pallas_call(
        functools.partial(layer_kernel, width),
        out_shape=jax.ShapeDtypeStruct((micros, model), BF16),
        in_specs=[in_vmem] * 5 + [anywhere] * 5,
        out_specs=in_vmem,
        scratch_shapes=[
            vmem((micros,) + keys.shape[2:], BF16),
            vmem((micros,) + values.shape[2:], BF16),
            vmem(w_router.shape[::-1], BF16),
            vmem((BLOCKS, blk, hidden), BF16),
            vmem((OUT_SLOTS, hidden, blk), BF16),
            vmem((4, micros, keys.shape[4]), jnp.int32),
            vmem((4, 4, head), F32),
            vmem((4, 4, head), F32),
            vmem((width, GROUPS, 16, piece), BF16),
            vmem((GROUPS * PIECES, rows, piece), BF16),
            vmem((rows, hidden), F32),
            vmem((rows, hidden), BF16),
            vmem((BLOCKS, rows // 2, blk), F32),
            vmem((BLOCKS, rows // 2, blk), BF16),
            vmem((BLOCKS, rows // 2, blk), BF16),
            vmem((GROUPS, chips, 16, piece), BF16),
            vmem((GROUPS, chips, 16, piece), BF16),
            dma((3,)),
            dma((BLOCKS,)),
            dma((BLOCKS,)),
            dma((4,)),
            dma((4,)),
            dma((4,)),
            dma((4,)),
            dma((2, chips)),
            dma((2, chips)),
            dma((2, chips)),
            dma((2, chips)),
            dma((BLOCKS,)),
            dma((BLOCKS,)),
            dma((GROUPS, chips)),
            dma((GROUPS, chips)),
        ],
        compiler_params=pltpu.CompilerParams(
            collective_id=0, has_side_effects=True, vmem_limit_bytes=61 * 1024 * 1024
        ),
    )(
        queries,
        lengths.T,
        routes,
        residual.reshape(micros, model),
        gain.reshape(model // HD, HD),
        keys.reshape((micros,) + keys.shape[2:]),
        values.reshape((micros,) + values.shape[2:]),
        w_router.T,
        w_in,
        w_out,
    ).reshape(residual.shape)


def solution(mesh):
    return jax.shard_map(
        on_device,
        mesh=mesh,
        in_specs=(
            P(None, ("grp", "ex"), None, None),
            P(None, ("grp", "ex"), None, None, None, None),
            P(None, ("grp", "ex"), None, None, None, None),
            P(None, ("grp", "ex")),
            P(None, ("grp", "ex"), None),
            P(None, ("grp", "ex"), None),
            P(),
            P(),
            P("ex", None, None),
            P("ex", None, None),
        ),
        out_specs=P(None, ("grp", "ex"), None),
        check_vma=False,
    )
```
